32 devices in a mesh: group: 2 (over x), module: 16 (over z, y, core).
Axes of the slice: x: 2, y: 2, z: 4, core: 2. Of those that a mesh axis runs over, the one named last changes fastest.
Arguments:
- query_grads: float32 [16, 32, 128, 128], P(None, None, 'module'), may hold values from -0.1875 to 0.1875
- train_grads: float32 [32, 128, 128, 128], P('module', 'group'), parts along dimension 1, may hold values from -0.1875 to 0.1875
- out_basis: float32 [32, 128, 128], P('module'), may hold values from -0.5 to 0.5
- in_basis: float32 [32, 128, 128], P('module'), may hold values from -0.5 to 0.5
- corrections: float32 [32, 128, 128], P('module'), may hold values from 0.01 to 10
- ranks: int32 [16], replicated, may hold values from 32 to 128
- slot_modules: int32 [32], replicated, may hold values from -1 to 15, as said below
Outputs:
- scores: float32 [32, 128], P(None, 'group'), parts along dimension 1
The draws below stay inside these ranges and needn't reach their ends.
There are 2 independent parts, one for each index of `group`. The reference program is written for one: setup_inputs(seed, part) draws one part's arguments, and reference() takes and returns one part's arrays. A program takes and returns all parts, laid end to end along the dimension named above; an argument that names none is the same for every part. Nothing has to cross between parts.
Inputs may be any that keep to these rules, and one draw needn't show every extreme that they name: `slot_modules`: each module number 0 to 15 stands in exactly one entry; all other entries are -1. Owner i holds the 2 entries from i * 2 on, so an owner holds 0 to 2 modules, and some owner holds 2.
All inputs are finite; a program needn't handle non-finite values.
Results may differ from the reference program's by a relative error of at most 0.0003.
Values sent between devices are 32-bit elements; how exact they have to be, the bound alone decides.
A program may use at most 128 MiB of HBM per device.

```python
import math
import jax
import jax.numpy as jnp
from jax import lax

DIM = 128
QUERIES = 32
EXAMPLES = 64
OWNER_SLOT_COUNT = 2
MODULES = 16
TOTAL_SLOT_ROWS = 32


def draw_slot_modules(key, part):
    order_key = jax.random.fold_in(key, 11)
    owner_key = jax.random.fold_in(key, 23)
    label_key = jax.random.fold_in(key, 37)
    ranking_keys = jax.random.permutation(order_key, TOTAL_SLOT_ROWS).astype(jnp.int32)
    selected_modules = jax.random.randint(owner_key, (), 0, TOTAL_SLOT_ROWS // OWNER_SLOT_COUNT)
    preference_boost = jnp.where(jnp.arange(TOTAL_SLOT_ROWS) // OWNER_SLOT_COUNT == selected_modules, TOTAL_SLOT_ROWS, 0).astype(jnp.int32)
    sorted_order = jnp.argsort(-(ranking_keys + preference_boost), stable=True)
    placement = jnp.argsort(sorted_order, stable=True).astype(jnp.int32)
    labels = jax.random.permutation(label_key, MODULES).astype(jnp.int32)
    picked = labels[jnp.clip(placement, 0, MODULES - 1)]
    return jnp.where(placement < MODULES, picked, -1).astype(jnp.int32)


def set_ends(drawn, stream_key, smallest, high):
    shape = drawn.shape
    index_at = [jax.random.randint(jax.random.fold_in(stream_key, axis), (), 0, shape[axis]) for axis in range(len(shape))]
    drawn = drawn.at[tuple(index_at)].set(smallest)
    longest = shape.index(max(shape))
    index_at[longest] = (index_at[longest] + 1) % shape[longest]
    return drawn.at[tuple(index_at)].set(high)


def levels(stream_key, extent, pieces, least, top_value):
    factor_of = 1.0
    for axis_at, shards_of in pieces:
        steps = jax.random.uniform(jax.random.fold_in(jax.random.fold_in(stream_key, 6), axis_at), (shards_of,), jnp.float32, least / len(pieces), top_value / len(pieces))
        factor_of = factor_of * jnp.repeat(jnp.exp(steps), extent[axis_at] // shards_of).reshape((-1,) + (1,) * (len(extent) - 1 - axis_at))
    return factor_of


def bell_draw(rng, shape, width, reach, cuts=(), held_as=jnp.bfloat16):
    gain = levels(rng, shape, cuts, -0.22, 0.18) if cuts else 1.0
    drawn = jax.random.normal(rng, shape, jnp.float32) * width * gain
    return jnp.minimum(jnp.maximum(drawn, -reach), reach).astype(held_as)


def setup_inputs(seed: int = 0, part: int = 0) -> dict:
    arg_keys = jax.random.split(jax.random.key(seed), 8)
    part_splits = jax.random.split(jax.random.fold_in(arg_keys[7], part), 8)
    query_grads = bell_draw(arg_keys[0], (MODULES, QUERIES, DIM, DIM), 0.03125, 0.1875, ((2, 16),), jnp.float32)
    train_grads = bell_draw(part_splits[1], (TOTAL_SLOT_ROWS, EXAMPLES, DIM, DIM), 0.03125, 0.1875, ((0, 16),), jnp.float32)
    out_basis = bell_draw(arg_keys[2], (TOTAL_SLOT_ROWS, DIM, DIM), DIM ** -0.5, 0.5, ((0, 16),), jnp.float32)
    in_basis = bell_draw(arg_keys[3], (TOTAL_SLOT_ROWS, DIM, DIM), DIM ** -0.5, 0.5, ((0, 16),), jnp.float32)
    corrections = jnp.clip(jnp.exp(math.log(10.0) - 6.9077553 * jax.random.uniform(arg_keys[4], (TOTAL_SLOT_ROWS, DIM, DIM), jnp.float32) ** levels(arg_keys[4], (TOTAL_SLOT_ROWS, DIM, DIM), ((0, 16),), -0.2, 0.2)), 0.01, 10.0)
    ranks = set_ends(jax.random.randint(arg_keys[5], (MODULES,), DIM // 4, DIM + 1), jax.random.fold_in(arg_keys[5], 1), DIM // 4, DIM).astype(jnp.int32)
    slot_modules = draw_slot_modules(jax.random.fold_in(arg_keys[7], 71), part)
    return dict(query_grads=query_grads, train_grads=train_grads, out_basis=out_basis, in_basis=in_basis, corrections=corrections, ranks=ranks, slot_modules=slot_modules)


def rotate(field, output_eigenbasis, inner_basis):
    inner = jnp.einsum('noi,ib->nob', field, inner_basis, precision=lax.Precision.HIGHEST)
    return jnp.einsum('oa,nob->nab', output_eigenbasis, inner, precision=lax.Precision.HIGHEST)


def slot_weight(spectrum, keep_rank):
    damping = 0.1 * jnp.mean(spectrum)
    positions = jnp.arange(spectrum.shape[0]).astype(jnp.int32)
    kept_mask = (positions[:, None] < keep_rank) & (positions[None, :] < keep_rank)
    return jnp.where(kept_mask, 1.0 / (spectrum + damping), jnp.zeros_like(spectrum))


def reference(query_grads, train_grads, out_basis, in_basis, corrections, ranks, slot_modules):
    def per_slot(running, inputs):
        module, train_block, output_eigenbasis, inner_basis, spectrum = inputs
        safe_index = jnp.maximum(module, 0)

        def occupied(unused):
            weight = slot_weight(spectrum, ranks[safe_index])
            scaled = rotate(query_grads[safe_index], output_eigenbasis, inner_basis) * weight
            rotated = rotate(train_block, output_eigenbasis, inner_basis)
            return jnp.einsum('qab,eab->qe', scaled, rotated, precision=lax.Precision.HIGHEST)

        def vacant(unused):
            return jnp.zeros((QUERIES, EXAMPLES), jnp.float32)

        return running + lax.cond(module >= 0, occupied, vacant, 0), None

    start = jnp.zeros((QUERIES, EXAMPLES), jnp.float32)
    running, unused = lax.scan(per_slot, start, (slot_modules, train_grads, out_basis, in_basis, corrections))
    return running
```

```python
import functools

import jax
import jax.numpy as jnp
from jax import lax
from jax.experimental import pallas as pl
from jax.experimental.pallas import tpu as pltpu
from jax.sharding import PartitionSpec as P

MESH = pl.DeviceIdType.MESH
F32 = jnp.float32
BF16 = jnp.bfloat16
PAIRS = 4


def split(x):
    high = x.astype(BF16)
    low = (x - high.astype(F32)).astype(BF16)
    return high, low


def halves_beside(x):
    high, low = split(x)
    return jnp.concatenate([high, low], axis=1)


def halves_below(x):
    high, low = split(x)
    return jnp.concatenate([high, low], axis=0)


def kernel(
    n, groups,
    slots_ref, ranks_ref, query_ref, train_ref, out_basis_ref, in_basis_ref, spectrum_ref,
    scores_ref,
    outgoing, received, train, left, right, weights, total, part, parts,
    train_sem, send_sem, recv_sem, pass_sem, passed_sem, sum_send_sem, sum_recv_sem,
):
    me = lax.axis_index("module")
    group = lax.axis_index("group")
    slots, dim = out_basis_ref.shape[0], out_basis_ref.shape[1]
    share, rows = received.shape[3], received.shape[4]
    examples = train_ref.shape[1] // dim
    queries = share * groups

    def peer(index):
        return (group, index)

    def group_peer(step):
        return (lax.rem(group + step, groups), me)

    load_train = [
        pltpu.make_async_copy(train_ref.at[k], train.at[k], train_sem.at[k]) for k in range(slots)
    ]
    for copy in load_train:
        copy.start()

    barrier = pltpu.get_barrier_semaphore()

    def greet(step, carry):
        pl.semaphore_signal(
            barrier, inc=1, device_id=peer(lax.rem(me + step, n)), device_id_type=MESH
        )
        return carry

    lax.fori_loop(1, n, greet, 0)
    for step in range(1, groups):
        pl.semaphore_signal(barrier, inc=1, device_id=group_peer(step), device_id_type=MESH)

    def offset(turn):
        return lax.rem(4 - lax.rem(turn, 4), 4) * (n // 4) + turn // 4

    def fill(turn, carry):
        target = lax.rem(me + offset(turn), n)
        for k in range(slots):
            module = jnp.maximum(slots_ref[target * slots + k], 0)
            outgoing[turn, k] = query_ref[module, pl.ds(group * share, share)]
        return carry

    lax.fori_loop(1, n, fill, 0)
    for k in range(slots):
        module = jnp.maximum(slots_ref[me * slots + k], 0)
        for g in range(groups):
            received[g, me, k] = query_ref[module, pl.ds(g * share, share)]

    pl.semaphore_wait(barrier, n - 1 + groups - 1)

    def message(turn, k):
        return pltpu.make_async_remote_copy(
            src_ref=outgoing.at[turn, k],
            dst_ref=received.at[group, me, k],
            send_sem=send_sem.at[turn, k],
            recv_sem=recv_sem.at[turn, k],
            device_id=peer(lax.rem(me + offset(turn), n)),
            device_id_type=MESH,
        )

    def send(turn, carry):
        for k in range(slots):
            message(turn, k).start()
        return carry

    lax.fori_loop(1, n, send, 0)

    def source(turn):
        return lax.rem(me + n - offset(turn), n)

    def arrival(turn, k):
        block = received.at[group, source(turn), k]
        return pltpu.make_async_remote_copy(
            src_ref=block,
            dst_ref=block,
            send_sem=send_sem.at[turn, k],
            recv_sem=recv_sem.at[turn, k],
            device_id=peer(source(turn)),
            device_id_type=MESH,
        )

    def hand_on(step, turn, k):
        block = received.at[group, source(turn), k]
        return pltpu.make_async_remote_copy(
            src_ref=block,
            dst_ref=block,
            send_sem=pass_sem.at[step, turn, k],
            recv_sem=passed_sem.at[step, turn, k],
            device_id=group_peer(step),
            device_id_type=MESH,
        )

    def handed(step, turn, k):
        giver = lax.rem(group + groups - step, groups)
        block = received.at[giver, source(turn), k]
        return pltpu.make_async_remote_copy(
            src_ref=block,
            dst_ref=block,
            send_sem=pass_sem.at[step, turn, k],
            recv_sem=passed_sem.at[step, turn, k],
            device_id=group_peer(step),
            device_id_type=MESH,
        )

    def turn_of(number):
        return number // slots + 1, lax.rem(number, slots)

    def forward(number):
        turn, k = turn_of(number)
        arrival(turn, k).wait_recv()
        for step in range(1, groups):
            hand_on(step, turn, k).start()

    for k in range(slots):
        u, v = out_basis_ref[k], in_basis_ref[k]
        for at, matrix in ((0, u.T), (1, u)):
            stacked = halves_below(matrix)
            left[k, at] = jnp.concatenate([stacked, stacked], axis=1)
        for at, matrix in ((0, v), (1, v.T)):
            beside = halves_beside(matrix)
            right[k, at] = jnp.concatenate([beside, beside], axis=0)
        module = slots_ref[me * slots + k]
        keep = jnp.where(module >= 0, ranks_ref[jnp.maximum(module, 0)], 0)
        spectrum = spectrum_ref[k]
        damping = 0.1 * jnp.mean(spectrum)
        kept = (lax.broadcasted_iota(jnp.int32, (dim, dim), 0) < keep) & (
            lax.broadcasted_iota(jnp.int32, (dim, dim), 1) < keep
        )
        weight = jnp.where(kept, 1.0 / (spectrum + damping), jnp.zeros_like(spectrum))
        weights[k] = jnp.concatenate([weight, weight], axis=1)

    def times_right(x, factor):
        product = jnp.dot(halves_beside(x), factor, preferred_element_type=F32)
        return product[:, :dim] + product[:, dim:]

    def times_left(factor, x):
        product = jnp.dot(factor, halves_below(x), preferred_element_type=F32)
        return product[:dim] + product[dim:]

    def side_by_side(x):
        return jnp.concatenate([x[:dim], x[dim:]], axis=1)

    def one_below_other(x):
        return jnp.concatenate([x[:, :dim], x[:, dim:]], axis=0)

    steps = examples // (2 * PAIRS)
    count = (n - 1) * slots
    early = min(count, steps * slots)

    for k in range(slots):
        load_train[k].wait()

        def rotate(step, carry, k=k):
            for pair in range(PAIRS):
                place = pl.ds((step * PAIRS + pair) * 2 * dim, 2 * dim)
                x = times_right(train[k, place], right[k, 0])
                x = times_left(left[k, 0], side_by_side(x)) * weights[k]
                x = times_right(one_below_other(x), right[k, 1])
                x = times_left(left[k, 1], side_by_side(x))
                train[k, place] = one_below_other(x)
            if early == steps * slots:
                forward(k * steps + step)
            return carry

        lax.fori_loop(0, steps, rotate, 0)

    if early != steps * slots:
        early = 0
    total[...] = jnp.zeros_like(total)

    def score(origin, k):
        added = jnp.zeros_like(total)
        for row in range(0, rows, 2):
            asked, given = [], []
            for r in (row, row + 1):
                block = jnp.concatenate(
                    [received[g, origin, k, :, r, :] for g in range(groups)], axis=0
                )
                asked.append(halves_below(block))
                taken = train[k, pl.ds(origin * rows + r, examples, stride=dim), :]
                given.append(halves_below(taken))
            added += lax.dot_general(
                jnp.concatenate(asked, axis=1),
                jnp.concatenate(given, axis=1),
                (((1,), (1,)), ((), ())),
                preferred_element_type=F32,
            )
        total[...] += added

    def use(number):
        turn, k = turn_of(number)
        for step in range(1, groups):
            handed(step, turn, k).wait_recv()
        score(source(turn), k)

    for k in range(slots):
        score(me, k)

    late = count - early
    twice = max(0, min(late, early - 2, count // 2))

    def both(i, carry):
        forward(early + i)
        use(2 * i)
        use(2 * i + 1)
        return carry

    lax.fori_loop(0, twice, both, 0)
    lag = early - twice
    if lag == 0 and late > twice:
        lag = 2
        for i in range(lag):
            forward(early + twice + i)
        begun = early + twice + lag
    else:
        begun = early + twice

    def single(number, carry):
        forward(number)
        use(number - lag)
        return carry

    lax.fori_loop(begun, count, single, 0)
    done = max(2 * twice, count - lag) if begun < count else 2 * twice

    def rest(number, carry):
        use(number)
        return carry

    lax.fori_loop(done, count, rest, 0)

    summed = total[...]
    summed = summed[:queries] + summed[queries:]
    summed = summed[:, :examples] + summed[:, examples:]
    half = queries // 2
    part[...] = jnp.concatenate([summed[:half], summed[half:]], axis=1)

    def partial(step):
        return pltpu.make_async_remote_copy(
            src_ref=part,
            dst_ref=parts.at[step],
            send_sem=sum_send_sem.at[step],
            recv_sem=sum_recv_sem.at[step],
            device_id=peer(lax.rem(me + step, n)),
            device_id_type=MESH,
        )

    def share_partial(step, carry):
        partial(step).start()
        return carry

    lax.fori_loop(1, n, share_partial, 0)
    parts[0] = part[...]

    def sent(turn, carry):
        for k in range(slots):
            message(turn, k).wait_send()
            for step in range(1, groups):
                hand_on(step, turn, k).wait_send()
        return carry

    lax.fori_loop(1, n, sent, 0)

    def arrived(step, carry):
        partial(step).wait_recv()
        return carry

    lax.fori_loop(1, n, arrived, 0)

    def add(owner, running):
        return running + parts[lax.rem(me + n - owner, n)]

    final = lax.fori_loop(0, n, add, jnp.zeros_like(part))
    scores_ref[...] = jnp.concatenate([final[:, :examples], final[:, examples:]], axis=0)

    def drained(step, carry):
        partial(step).wait_send()
        return carry

    lax.fori_loop(1, n, drained, 0)


def body(n, groups, query_grads, train_grads, out_basis, in_basis, corrections, ranks, slot_modules):
    modules, queries, rows, dim = query_grads.shape
    slots, examples = train_grads.shape[:2]
    share = queries // groups
    vmem = pl.BlockSpec(memory_space=pltpu.VMEM)
    smem = pl.BlockSpec(memory_space=pltpu.SMEM)
    return pl.pallas_call(
        functools.partial(kernel, n, groups),
        out_shape=jax.ShapeDtypeStruct((queries, examples), F32),
        in_specs=[smem, smem, vmem, pl.BlockSpec(memory_space=pl.ANY), vmem, vmem, vmem],
        out_specs=vmem,
        scratch_shapes=[
            pltpu.VMEM((n, slots, share, rows, dim), F32),
            pltpu.VMEM((groups, n, slots, share, rows, dim), F32),
            pltpu.VMEM((slots, examples * dim, dim), F32),
            pltpu.VMEM((slots, 2, 2 * dim, 2 * dim), BF16),
            pltpu.VMEM((slots, 2, 2 * dim, 2 * dim), BF16),
            pltpu.VMEM((slots, dim, 2 * dim), F32),
            pltpu.VMEM((2 * queries, 2 * examples), F32),
            pltpu.VMEM((queries // 2, 2 * examples), F32),
            pltpu.VMEM((n, queries // 2, 2 * examples), F32),
            pltpu.SemaphoreType.DMA((slots,)),
            pltpu.SemaphoreType.DMA((n, slots)),
            pltpu.SemaphoreType.DMA((n, slots)),
            pltpu.SemaphoreType.DMA((groups, n, slots)),
            pltpu.SemaphoreType.DMA((groups, n, slots)),
            pltpu.SemaphoreType.DMA((n,)),
            pltpu.SemaphoreType.DMA((n,)),
        ],
        compiler_params=pltpu.CompilerParams(
            collective_id=0, has_side_effects=True, vmem_limit_bytes=48 * 1024 * 1024
        ),
    )(
        slot_modules, ranks, query_grads, train_grads.reshape(slots, examples * dim, dim),
        out_basis, in_basis, corrections,
    )


def solution(mesh):
    return jax.shard_map(
        functools.partial(body, mesh.shape["module"], mesh.shape["group"]),
        mesh=mesh,
        in_specs=(
            P(None, None, "module", None),
            P("module", "group", None, None),
            P("module", None, None),
            P("module", None, None),
            P("module", None, None),
            P(),
            P(),
        ),
        out_specs=P(None, "group"),
        check_vma=False,
    )
```

```python
import functools

import jax
import jax.numpy as jnp
from jax import lax
from jax.experimental import pallas as pl
from jax.experimental.pallas import tpu as pltpu
from jax.sharding import PartitionSpec as P

MESH = pl.DeviceIdType.MESH
F32 = jnp.float32
BF16 = jnp.bfloat16
PAIRS = 4


def split(x):
    high = x.astype(BF16)
    low = (x - high.astype(F32)).astype(BF16)
    return high, low


def halves_beside(x):
    high, low = split(x)
    return jnp.concatenate([high, low], axis=1)


def halves_below(x):
    high, low = split(x)
    return jnp.concatenate([high, low], axis=0)


def kernel(
    n, groups,
    slots_hbm, ranks_hbm, query_hbm, train_ref, out_basis_hbm, in_basis_hbm, spectrum_hbm,
    scores_ref,
    slots_ref, ranks_ref, query_ref, out_basis_ref, in_basis_ref, spectrum_ref,
    outgoing, direct, received, train, left, right, weights, total, part, parts,
    load_sem, train_sem, send_sem, recv_sem, direct_send_sem, direct_recv_sem, pass_sem, passed_sem, sum_send_sem, sum_recv_sem,
):
    me = lax.axis_index("module")
    group = lax.axis_index("group")
    slots, dim = out_basis_ref.shape[0], out_basis_ref.shape[1]
    share, rows = received.shape[3], received.shape[4]
    part_size = n // 2
    examples = train_ref.shape[1] // dim
    queries = share * groups

    def peer(index):
        return (group, index)

    def group_peer(step):
        return (lax.rem(group + step, groups), me)

    loads = [
        pltpu.make_async_copy(source_ref, target_ref, load_sem.at[at])
        for at, (source_ref, target_ref) in enumerate(
            (
                (slots_hbm, slots_ref),
                (query_hbm, query_ref),
                (ranks_hbm, ranks_ref),
                (out_basis_hbm, out_basis_ref),
                (in_basis_hbm, in_basis_ref),
                (spectrum_hbm, spectrum_ref),
            )
        )
    ]
    for copy in loads:
        copy.start()

    barrier = pltpu.get_barrier_semaphore()

    def greet(step, carry):
        pl.semaphore_signal(
            barrier, inc=1, device_id=peer(lax.rem(me + step, n)), device_id_type=MESH
        )
        return carry

    lax.fori_loop(1, n, greet, 0)
    for step in range(1, groups):
        pl.semaphore_signal(barrier, inc=1, device_id=group_peer(step), device_id_type=MESH)

    load_train = [
        pltpu.make_async_copy(train_ref.at[k], train.at[k], train_sem.at[k]) for k in range(slots)
    ]
    for copy in load_train:
        copy.start()

    mine = me // part_size
    place = lax.rem(me, part_size)

    def across(turn):
        return (1 - mine) * part_size + lax.rem(place + turn, part_size)

    def within(turn):
        return mine * part_size + lax.rem(place + turn, part_size)

    def source(turn):
        return (1 - mine) * part_size + lax.rem(place + part_size - turn, part_size)

    def near_source(turn):
        return mine * part_size + lax.rem(place + part_size - turn, part_size)

    def wanted(target, k):
        return jnp.maximum(slots_ref[target * slots + k], 0)

    loads[0].wait()
    loads[1].wait()

    def fill(turn, carry):
        for k in range(slots):
            outgoing[turn, k] = query_ref[wanted(across(turn), k), pl.ds(group * share, share)]
        return carry

    lax.fori_loop(0, part_size, fill, 0)
    pl.semaphore_wait(barrier, n - 1 + groups - 1)

    def message(turn, k):
        return pltpu.make_async_remote_copy(
            src_ref=outgoing.at[turn, k],
            dst_ref=received.at[me, k, group],
            send_sem=send_sem.at[turn, k],
            recv_sem=recv_sem.at[turn, k],
            device_id=peer(across(turn)),
            device_id_type=MESH,
        )

    def near_message(turn, k):
        return pltpu.make_async_remote_copy(
            src_ref=direct.at[turn, k],
            dst_ref=received.at[me, k],
            send_sem=direct_send_sem.at[turn, k],
            recv_sem=direct_recv_sem.at[turn, k],
            device_id=peer(within(turn)),
            device_id_type=MESH,
        )

    def send(turn, carry):
        for k in range(slots):
            message(turn, k).start()
        return carry

    lax.fori_loop(0, part_size, send, 0)

    def send_near(turn, carry):
        for k in range(slots):
            for g in range(groups):
                direct[turn, k, g] = query_ref[wanted(within(turn), k), pl.ds(g * share, share)]
            near_message(turn, k).start()
        return carry

    lax.fori_loop(1, part_size, send_near, 0)
    for k in range(slots):
        for g in range(groups):
            received[me, k, g] = query_ref[wanted(me, k), pl.ds(g * share, share)]

    def arrival(turn, k):
        block = received.at[source(turn), k, group]
        return pltpu.make_async_remote_copy(
            src_ref=block,
            dst_ref=block,
            send_sem=send_sem.at[turn, k],
            recv_sem=recv_sem.at[turn, k],
            device_id=peer(source(turn)),
            device_id_type=MESH,
        )

    def near_arrival(turn, k):
        block = received.at[near_source(turn), k]
        return pltpu.make_async_remote_copy(
            src_ref=block,
            dst_ref=block,
            send_sem=direct_send_sem.at[turn, k],
            recv_sem=direct_recv_sem.at[turn, k],
            device_id=peer(near_source(turn)),
            device_id_type=MESH,
        )

    def hand_on(step, turn, k):
        block = received.at[source(turn), k, group]
        return pltpu.make_async_remote_copy(
            src_ref=block,
            dst_ref=block,
            send_sem=pass_sem.at[step, turn, k],
            recv_sem=passed_sem.at[step, turn, k],
            device_id=group_peer(step),
            device_id_type=MESH,
        )

    def handed(step, turn, k):
        giver = lax.rem(group + groups - step, groups)
        block = received.at[source(turn), k, giver]
        return pltpu.make_async_remote_copy(
            src_ref=block,
            dst_ref=block,
            send_sem=pass_sem.at[step, turn, k],
            recv_sem=passed_sem.at[step, turn, k],
            device_id=group_peer(step),
            device_id_type=MESH,
        )

    def turn_of(number):
        return number // slots, lax.rem(number, slots)

    def forward(number):
        turn, k = turn_of(number)
        arrival(turn, k).wait_recv()
        for step in range(1, groups):
            hand_on(step, turn, k).start()

    for copy in loads[2:]:
        copy.wait()

    for k in range(slots):
        u, v = out_basis_ref[k], in_basis_ref[k]
        for at, matrix in ((0, u.T), (1, u)):
            stacked = halves_below(matrix)
            left[k, at] = jnp.concatenate([stacked, stacked], axis=1)
        for at, matrix in ((0, v), (1, v.T)):
            beside = halves_beside(matrix)
            right[k, at] = jnp.concatenate([beside, beside], axis=0)
        module = slots_ref[me * slots + k]
        keep = jnp.where(module >= 0, ranks_ref[jnp.maximum(module, 0)], 0)
        spectrum = spectrum_ref[k]
        damping = 0.1 * jnp.mean(spectrum)
        kept = (lax.broadcasted_iota(jnp.int32, (dim, dim), 0) < keep) & (
            lax.broadcasted_iota(jnp.int32, (dim, dim), 1) < keep
        )
        weight = jnp.where(kept, 1.0 / (spectrum + damping), jnp.zeros_like(spectrum))
        weights[k] = jnp.concatenate([weight, weight], axis=1)

    def times_right(x, factor):
        product = jnp.dot(halves_beside(x), factor, preferred_element_type=F32)
        return product[:, :dim] + product[:, dim:]

    def times_left(factor, x):
        product = jnp.dot(factor, halves_below(x), preferred_element_type=F32)
        return product[:dim] + product[dim:]

    def side_by_side(x):
        return jnp.concatenate([x[:dim], x[dim:]], axis=1)

    def one_below_other(x):
        return jnp.concatenate([x[:, :dim], x[:, dim:]], axis=0)

    steps = examples // (2 * PAIRS)
    count = part_size * slots
    early = steps // 2 + (slots - 1) * steps

    for k in range(slots):
        load_train[k].wait()

        def rotate(step, carry, k=k):
            for pair in range(PAIRS):
                place = pl.ds((step * PAIRS + pair) * 2 * dim, 2 * dim)
                x = times_right(train[k, place], right[k, 0])
                x = times_left(left[k, 0], side_by_side(x)) * weights[k]
                x = times_right(one_below_other(x), right[k, 1])
                x = times_left(left[k, 1], side_by_side(x))
                train[k, place] = one_below_other(x)
            if k == 0:
                pl.when(lax.rem(step, 2) == 1)(lambda: forward(step // 2))
            else:
                forward(steps // 2 + (k - 1) * steps + step)
            return carry

        lax.fori_loop(0, steps, rotate, 0)

    total[...] = jnp.zeros_like(total)

    def score(origin, k):
        added = jnp.zeros_like(total)
        for row in range(0, rows, 2):
            asked, given = [], []
            for r in (row, row + 1):
                block = jnp.concatenate(
                    [received[origin, k, g, :, r, :] for g in range(groups)], axis=0
                )
                asked.append(halves_below(block))
                taken = train[k, pl.ds(origin * rows + r, examples, stride=dim), :]
                given.append(halves_below(taken))
            added += lax.dot_general(
                jnp.concatenate(asked, axis=1),
                jnp.concatenate(given, axis=1),
                (((1,), (1,)), ((), ())),
                preferred_element_type=F32,
            )
        total[...] += added

    def use(number):
        turn, k = turn_of(number)
        for step in range(1, groups):
            handed(step, turn, k).wait_recv()
        score(source(turn), k)

    for k in range(slots):
        score(me, k)

    late = count - early
    each = min(early // late, 3)
    near_count = (part_size - 1) * slots

    def use_near(number):
        turn, k = turn_of(number + slots)
        near_arrival(turn, k).wait_recv()
        score(near_source(turn), k)

    def late_forward(number, carry):
        forward(early + number)
        for at in range(each):
            use(each * number + at)
            if each == 3:
                use_near(each * number + at)
        return carry

    def near_only(number, carry):
        use_near(number)
        return carry

    def rest(number, carry):
        use(number)
        return carry

    lax.fori_loop(0, late, late_forward, 0)
    lax.fori_loop(late * each if each == 3 else 0, near_count, near_only, 0)
    lax.fori_loop(each * late, count, rest, 0)

    summed = total[...]
    summed = summed[:queries] + summed[queries:]
    summed = summed[:, :examples] + summed[:, examples:]
    half = queries // 2
    part[...] = jnp.concatenate([summed[:half], summed[half:]], axis=1)

    def partial(step):
        return pltpu.make_async_remote_copy(
            src_ref=part,
            dst_ref=parts.at[step],
            send_sem=sum_send_sem.at[step],
            recv_sem=sum_recv_sem.at[step],
            device_id=peer(lax.rem(me + step, n)),
            device_id_type=MESH,
        )

    def share_partial(step, carry):
        partial(step).start()
        return carry

    lax.fori_loop(1, n, share_partial, 0)
    parts[0] = part[...]

    def arrived(step, carry):
        partial(step).wait_recv()
        return carry

    lax.fori_loop(1, n, arrived, 0)

    def add(owner, running):
        return running + parts[lax.rem(me + n - owner, n)]

    final = lax.fori_loop(0, n, add, jnp.zeros_like(part))
    scores_ref[...] = jnp.concatenate([final[:, :examples], final[:, examples:]], axis=0)

    def drained(step, carry):
        partial(step).wait_send()
        return carry

    lax.fori_loop(1, n, drained, 0)

    def sent(turn, carry):
        for k in range(slots):
            message(turn, k).wait_send()
            for step in range(1, groups):
                hand_on(step, turn, k).wait_send()
        return carry

    def near_sent(turn, carry):
        for k in range(slots):
            near_message(turn, k).wait_send()
        return carry

    lax.fori_loop(0, part_size, sent, 0)
    lax.fori_loop(1, part_size, near_sent, 0)


def body(n, groups, query_grads, train_grads, out_basis, in_basis, corrections, ranks, slot_modules):
    modules, queries, rows, dim = query_grads.shape
    slots, examples = train_grads.shape[:2]
    share = queries // groups
    vmem = pl.BlockSpec(memory_space=pltpu.VMEM)
    hbm = pl.BlockSpec(memory_space=pltpu.HBM)
    return pl.pallas_call(
        functools.partial(kernel, n, groups),
        out_shape=jax.ShapeDtypeStruct((queries, examples), F32),
        in_specs=[hbm] * 7,
        out_specs=vmem,
        scratch_shapes=[
            pltpu.SMEM(slot_modules.shape, jnp.int32),
            pltpu.SMEM(ranks.shape, jnp.int32),
            pltpu.VMEM(query_grads.shape, F32),
            pltpu.VMEM(out_basis.shape, F32),
            pltpu.VMEM(in_basis.shape, F32),
            pltpu.VMEM(corrections.shape, F32),
            pltpu.VMEM((n // 2, slots, share, rows, dim), F32),
            pltpu.VMEM((n // 2, slots, groups, share, rows, dim), F32),
            pltpu.VMEM((n, slots, groups, share, rows, dim), F32),
            pltpu.VMEM((slots, examples * dim, dim), F32),
            pltpu.VMEM((slots, 2, 2 * dim, 2 * dim), BF16),
            pltpu.VMEM((slots, 2, 2 * dim, 2 * dim), BF16),
            pltpu.VMEM((slots, dim, 2 * dim), F32),
            pltpu.VMEM((2 * queries, 2 * examples), F32),
            pltpu.VMEM((queries // 2, 2 * examples), F32),
            pltpu.VMEM((n, queries // 2, 2 * examples), F32),
            pltpu.SemaphoreType.DMA((6,)),
            pltpu.SemaphoreType.DMA((slots,)),
            pltpu.SemaphoreType.DMA((n // 2, slots)),
            pltpu.SemaphoreType.DMA((n // 2, slots)),
            pltpu.SemaphoreType.DMA((n // 2, slots)),
            pltpu.SemaphoreType.DMA((n // 2, slots)),
            pltpu.SemaphoreType.DMA((groups, n // 2, slots)),
            pltpu.SemaphoreType.DMA((groups, n // 2, slots)),
            pltpu.SemaphoreType.DMA((n,)),
            pltpu.SemaphoreType.DMA((n,)),
        ],
        compiler_params=pltpu.CompilerParams(
            collective_id=0, has_side_effects=True, vmem_limit_bytes=64 * 1024 * 1024
        ),
    )(
        slot_modules, ranks, query_grads, train_grads.reshape(slots, examples * dim, dim),
        out_basis, in_basis, corrections,
    )


def solution(mesh):
    return jax.shard_map(
        functools.partial(body, mesh.shape["module"], mesh.shape["group"]),
        mesh=mesh,
        in_specs=(
            P(None, None, "module", None),
            P("module", "group", None, None),
            P("module", None, None),
            P("module", None, None),
            P("module", None, None),
            P(),
            P(),
        ),
        out_specs=P(None, "group"),
        check_vma=False,
    )
```

```python
import functools

import jax
import jax.numpy as jnp
from jax import lax
from jax.experimental import pallas as pl
from jax.experimental.pallas import tpu as pltpu
from jax.sharding import PartitionSpec as P

MESH = pl.DeviceIdType.MESH
F32 = jnp.float32
BF16 = jnp.bfloat16
PAIRS = 4


def split(x):
    high = x.astype(BF16)
    low = (x - high.astype(F32)).astype(BF16)
    return high, low


def halves_beside(x):
    high, low = split(x)
    return jnp.concatenate([high, low], axis=1)


def halves_below(x):
    high, low = split(x)
    return jnp.concatenate([high, low], axis=0)


def kernel(
    n, groups,
    slots_hbm, ranks_hbm, query_hbm, train_ref, out_basis_hbm, in_basis_hbm, spectrum_hbm,
    scores_ref,
    slots_ref, ranks_ref, query_ref, out_basis_ref, in_basis_ref, spectrum_ref,
    outgoing, direct, received, train, left, right, weights, total, part, parts,
    load_sem, train_sem, send_sem, recv_sem, direct_send_sem, direct_recv_sem, pass_sem, passed_sem, sum_send_sem, sum_recv_sem,
):
    me = lax.axis_index("module")
    group = lax.axis_index("group")
    slots, dim = out_basis_ref.shape[0], out_basis_ref.shape[1]
    share, rows = received.shape[3], received.shape[4]
    part_size = n // 2
    examples = train_ref.shape[1] // dim
    queries = share * groups

    def peer(index):
        return (group, index)

    def group_peer(step):
        return (lax.rem(group + step, groups), me)

    loads = [
        pltpu.make_async_copy(source_ref, target_ref, load_sem.at[at])
        for at, (source_ref, target_ref) in enumerate(
            (
                (slots_hbm, slots_ref),
                (query_hbm, query_ref),
                (ranks_hbm, ranks_ref),
                (out_basis_hbm, out_basis_ref),
                (in_basis_hbm, in_basis_ref),
                (spectrum_hbm, spectrum_ref),
            )
        )
    ]
    for copy in loads:
        copy.start()

    barrier = pltpu.get_barrier_semaphore()

    def greet(step, carry):
        pl.semaphore_signal(
            barrier, inc=1, device_id=peer(lax.rem(me + step, n)), device_id_type=MESH
        )
        return carry

    lax.fori_loop(1, n, greet, 0)
    for step in range(1, groups):
        pl.semaphore_signal(barrier, inc=1, device_id=group_peer(step), device_id_type=MESH)

    load_train = [
        pltpu.make_async_copy(train_ref.at[k], train.at[k], train_sem.at[k]) for k in range(slots)
    ]
    for copy in load_train:
        copy.start()

    mine = me // part_size
    place = lax.rem(me, part_size)

    def across(turn):
        return (1 - mine) * part_size + lax.rem(place + turn, part_size)

    def within(turn):
        return mine * part_size + lax.rem(place + turn, part_size)

    def source(turn):
        return (1 - mine) * part_size + lax.rem(place + part_size - turn, part_size)

    def near_source(turn):
        return mine * part_size + lax.rem(place + part_size - turn, part_size)

    def wanted(target, k):
        return jnp.maximum(slots_ref[target * slots + k], 0)

    loads[0].wait()
    loads[1].wait()

    def fill(turn, carry):
        for k in range(slots):
            outgoing[turn, k] = query_ref[wanted(across(turn), k), pl.ds(group * share, share)]
        return carry

    lax.fori_loop(0, part_size, fill, 0)
    pl.semaphore_wait(barrier, n - 1 + groups - 1)

    def message(turn, k):
        return pltpu.make_async_remote_copy(
            src_ref=outgoing.at[turn, k],
            dst_ref=received.at[me, k, group],
            send_sem=send_sem.at[turn, k],
            recv_sem=recv_sem.at[turn, k],
            device_id=peer(across(turn)),
            device_id_type=MESH,
        )

    def near_message(turn, k):
        return pltpu.make_async_remote_copy(
            src_ref=direct.at[turn, k],
            dst_ref=received.at[me, k],
            send_sem=direct_send_sem.at[turn, k],
            recv_sem=direct_recv_sem.at[turn, k],
            device_id=peer(within(turn)),
            device_id_type=MESH,
        )

    def send(turn, carry):
        for k in range(slots):
            message(turn, k).start()
        return carry

    def send_near(turn, carry):
        for k in range(slots):
            for g in range(groups):
                direct[turn, k, g] = query_ref[wanted(within(turn), k), pl.ds(g * share, share)]
            near_message(turn, k).start()
            message(turn, k).start()
        return carry

    send(0, 0)
    lax.fori_loop(1, part_size, send_near, 0)
    for k in range(slots):
        for g in range(groups):
            received[me, k, g] = query_ref[wanted(me, k), pl.ds(g * share, share)]

    def arrival(turn, k):
        block = received.at[source(turn), k, group]
        return pltpu.make_async_remote_copy(
            src_ref=block,
            dst_ref=block,
            send_sem=send_sem.at[turn, k],
            recv_sem=recv_sem.at[turn, k],
            device_id=peer(source(turn)),
            device_id_type=MESH,
        )

    def near_arrival(turn, k):
        block = received.at[near_source(turn), k]
        return pltpu.make_async_remote_copy(
            src_ref=block,
            dst_ref=block,
            send_sem=direct_send_sem.at[turn, k],
            recv_sem=direct_recv_sem.at[turn, k],
            device_id=peer(near_source(turn)),
            device_id_type=MESH,
        )

    def hand_on(step, turn, k):
        block = received.at[source(turn), k, group]
        return pltpu.make_async_remote_copy(
            src_ref=block,
            dst_ref=block,
            send_sem=pass_sem.at[step, turn, k],
            recv_sem=passed_sem.at[step, turn, k],
            device_id=group_peer(step),
            device_id_type=MESH,
        )

    def handed(step, turn, k):
        giver = lax.rem(group + groups - step, groups)
        block = received.at[source(turn), k, giver]
        return pltpu.make_async_remote_copy(
            src_ref=block,
            dst_ref=block,
            send_sem=pass_sem.at[step, turn, k],
            recv_sem=passed_sem.at[step, turn, k],
            device_id=group_peer(step),
            device_id_type=MESH,
        )

    def turn_of(number):
        return number // slots, lax.rem(number, slots)

    def forward(number):
        turn, k = turn_of(number)
        arrival(turn, k).wait_recv()
        for step in range(1, groups):
            hand_on(step, turn, k).start()

    for copy in loads[2:]:
        copy.wait()

    for k in range(slots):
        u, v = out_basis_ref[k], in_basis_ref[k]
        for at, matrix in ((0, u.T), (1, u)):
            stacked = halves_below(matrix)
            left[k, at] = jnp.concatenate([stacked, stacked], axis=1)
        for at, matrix in ((0, v), (1, v.T)):
            beside = halves_beside(matrix)
            right[k, at] = jnp.concatenate([beside, beside], axis=0)
        module = slots_ref[me * slots + k]
        keep = jnp.where(module >= 0, ranks_ref[jnp.maximum(module, 0)], 0)
        spectrum = spectrum_ref[k]
        damping = 0.1 * jnp.mean(spectrum)
        kept = (lax.broadcasted_iota(jnp.int32, (dim, dim), 0) < keep) & (
            lax.broadcasted_iota(jnp.int32, (dim, dim), 1) < keep
        )
        weight = jnp.where(kept, 1.0 / (spectrum + damping), jnp.zeros_like(spectrum))
        weights[k] = jnp.concatenate([weight, weight], axis=1)

    def times_right(x, factor):
        product = jnp.dot(halves_beside(x), factor, preferred_element_type=F32)
        return product[:, :dim] + product[:, dim:]

    def times_left(factor, x):
        product = jnp.dot(factor, halves_below(x), preferred_element_type=F32)
        return product[:dim] + product[dim:]

    def side_by_side(x):
        return jnp.concatenate([x[:dim], x[dim:]], axis=1)

    def one_below_other(x):
        return jnp.concatenate([x[:, :dim], x[:, dim:]], axis=0)

    steps = examples // (2 * PAIRS)
    count = part_size * slots
    early = steps // 2 + (slots - 1) * steps

    for k in range(slots):
        load_train[k].wait()

        def rotate(step, carry, k=k):
            for pair in range(PAIRS):
                place = pl.ds((step * PAIRS + pair) * 2 * dim, 2 * dim)
                x = times_right(train[k, place], right[k, 0])
                x = times_left(left[k, 0], side_by_side(x)) * weights[k]
                x = times_right(one_below_other(x), right[k, 1])
                x = times_left(left[k, 1], side_by_side(x))
                train[k, place] = one_below_other(x)
            if k == 0:
                pl.when(lax.rem(step, 2) == 1)(lambda: forward(step // 2))
            else:
                forward(steps // 2 + (k - 1) * steps + step)
            return carry

        lax.fori_loop(0, steps, rotate, 0)

    total[...] = jnp.zeros_like(total)

    def score(origin, k):
        added = jnp.zeros_like(total)
        for row in range(0, rows, 2):
            asked, given = [], []
            for r in (row, row + 1):
                block = jnp.concatenate(
                    [received[origin, k, g, :, r, :] for g in range(groups)], axis=0
                )
                asked.append(halves_below(block))
                taken = train[k, pl.ds(origin * rows + r, examples, stride=dim), :]
                given.append(halves_below(taken))
            added += lax.dot_general(
                jnp.concatenate(asked, axis=1),
                jnp.concatenate(given, axis=1),
                (((1,), (1,)), ((), ())),
                preferred_element_type=F32,
            )
        total[...] += added

    def use(number):
        turn, k = turn_of(number)
        for step in range(1, groups):
            handed(step, turn, k).wait_recv()
        score(source(turn), k)

    for k in range(slots):
        score(me, k)

    late = count - early
    each = min(early // late, 3)
    near_count = (part_size - 1) * slots

    def use_near(number):
        turn, k = turn_of(number + slots)
        near_arrival(turn, k).wait_recv()
        score(near_source(turn), k)

    def late_forward(number, carry):
        forward(early + number)
        for at in range(each):
            use(each * number + at)
            if each == 3:
                use_near(each * number + at)
        return carry

    def near_only(number, carry):
        use_near(number)
        return carry

    def rest(number, carry):
        use(number)
        return carry

    lax.fori_loop(0, late, late_forward, 0)
    lax.fori_loop(late * each if each == 3 else 0, near_count, near_only, 0)
    lax.fori_loop(each * late, count, rest, 0)

    summed = total[...]
    summed = summed[:queries] + summed[queries:]
    summed = summed[:, :examples] + summed[:, examples:]
    half = queries // 2
    part[...] = jnp.concatenate([summed[:half], summed[half:]], axis=1)

    def partial(step):
        return pltpu.make_async_remote_copy(
            src_ref=part,
            dst_ref=parts.at[step],
            send_sem=sum_send_sem.at[step],
            recv_sem=sum_recv_sem.at[step],
            device_id=peer(lax.rem(me + step, n)),
            device_id_type=MESH,
        )

    def share_partial(step, carry):
        partial(step).start()
        return carry

    lax.fori_loop(1, n, share_partial, 0)
    parts[0] = part[...]

    def arrived(step, carry):
        partial(step).wait_recv()
        return carry

    lax.fori_loop(1, n, arrived, 0)

    def add(owner, running):
        return running + parts[lax.rem(me + n - owner, n)]

    final = lax.fori_loop(0, n, add, jnp.zeros_like(part))
    scores_ref[...] = jnp.concatenate([final[:, :examples], final[:, examples:]], axis=0)

    def drained(step, carry):
        partial(step).wait_send()
        return carry

    lax.fori_loop(1, n, drained, 0)

    def sent(turn, carry):
        for k in range(slots):
            message(turn, k).wait_send()
            for step in range(1, groups):
                hand_on(step, turn, k).wait_send()
        return carry

    def near_sent(turn, carry):
        for k in range(slots):
            near_message(turn, k).wait_send()
        return carry

    lax.fori_loop(0, part_size, sent, 0)
    lax.fori_loop(1, part_size, near_sent, 0)


def body(n, groups, query_grads, train_grads, out_basis, in_basis, corrections, ranks, slot_modules):
    modules, queries, rows, dim = query_grads.shape
    slots, examples = train_grads.shape[:2]
    share = queries // groups
    vmem = pl.BlockSpec(memory_space=pltpu.VMEM)
    hbm = pl.BlockSpec(memory_space=pltpu.HBM)
    return pl.pallas_call(
        functools.partial(kernel, n, groups),
        out_shape=jax.ShapeDtypeStruct((queries, examples), F32),
        in_specs=[hbm] * 7,
        out_specs=vmem,
        scratch_shapes=[
            pltpu.SMEM(slot_modules.shape, jnp.int32),
            pltpu.SMEM(ranks.shape, jnp.int32),
            pltpu.VMEM(query_grads.shape, F32),
            pltpu.VMEM(out_basis.shape, F32),
            pltpu.VMEM(in_basis.shape, F32),
            pltpu.VMEM(corrections.shape, F32),
            pltpu.VMEM((n // 2, slots, share, rows, dim), F32),
            pltpu.VMEM((n // 2, slots, groups, share, rows, dim), F32),
            pltpu.VMEM((n, slots, groups, share, rows, dim), F32),
            pltpu.VMEM((slots, examples * dim, dim), F32),
            pltpu.VMEM((slots, 2, 2 * dim, 2 * dim), BF16),
            pltpu.VMEM((slots, 2, 2 * dim, 2 * dim), BF16),
            pltpu.VMEM((slots, dim, 2 * dim), F32),
            pltpu.VMEM((2 * queries, 2 * examples), F32),
            pltpu.VMEM((queries // 2, 2 * examples), F32),
            pltpu.VMEM((n, queries // 2, 2 * examples), F32),
            pltpu.SemaphoreType.DMA((6,)),
            pltpu.SemaphoreType.DMA((slots,)),
            pltpu.SemaphoreType.DMA((n // 2, slots)),
            pltpu.SemaphoreType.DMA((n // 2, slots)),
            pltpu.SemaphoreType.DMA((n // 2, slots)),
            pltpu.SemaphoreType.DMA((n // 2, slots)),
            pltpu.SemaphoreType.DMA((groups, n // 2, slots)),
            pltpu.SemaphoreType.DMA((groups, n // 2, slots)),
            pltpu.SemaphoreType.DMA((n,)),
            pltpu.SemaphoreType.DMA((n,)),
        ],
        compiler_params=pltpu.CompilerParams(
            collective_id=0, has_side_effects=True, vmem_limit_bytes=64 * 1024 * 1024
        ),
    )(
        slot_modules, ranks, query_grads, train_grads.reshape(slots, examples * dim, dim),
        out_basis, in_basis, corrections,
    )


def solution(mesh):
    return jax.shard_map(
        functools.partial(body, mesh.shape["module"], mesh.shape["group"]),
        mesh=mesh,
        in_specs=(
            P(None, None, "module", None),
            P("module", "group", None, None),
            P("module", None, None),
            P("module", None, None),
            P("module", None, None),
            P(),
            P(),
        ),
        out_specs=P(None, "group"),
        check_vma=False,
    )
```

```python
import functools

import jax
import jax.numpy as jnp
from jax import lax
from jax.experimental import pallas as pl
from jax.experimental.pallas import tpu as pltpu
from jax.sharding import PartitionSpec as P

MESH = pl.DeviceIdType.MESH
F32 = jnp.float32
BF16 = jnp.bfloat16
PAIRS = 4


def split(x):
    high = x.astype(BF16)
    low = (x - high.astype(F32)).astype(BF16)
    return high, low


def halves_beside(x):
    high, low = split(x)
    return jnp.concatenate([high, low], axis=1)


def halves_below(x):
    high, low = split(x)
    return jnp.concatenate([high, low], axis=0)


def kernel(
    n, groups,
    slots_hbm, ranks_hbm, query_hbm, train_ref, out_basis_hbm, in_basis_hbm, spectrum_hbm,
    scores_ref,
    slots_ref, ranks_ref, query_ref, out_basis_ref, in_basis_ref, spectrum_ref,
    outgoing, direct, received, train, left, right, weights, total, part, parts,
    load_sem, train_sem, send_sem, recv_sem, direct_send_sem, direct_recv_sem, pass_sem, passed_sem, sum_send_sem, sum_recv_sem,
):
    me = lax.axis_index("module")
    group = lax.axis_index("group")
    slots, dim = out_basis_ref.shape[0], out_basis_ref.shape[1]
    share, rows = received.shape[3], received.shape[4]
    part_size = n // 2
    examples = train_ref.shape[1] // dim
    queries = share * groups

    def peer(index):
        return (group, index)

    def group_peer(step):
        return (lax.rem(group + step, groups), me)

    loads = [
        pltpu.make_async_copy(source_ref, target_ref, load_sem.at[at])
        for at, (source_ref, target_ref) in enumerate(
            (
                (slots_hbm, slots_ref),
                (query_hbm, query_ref),
                (ranks_hbm, ranks_ref),
                (out_basis_hbm, out_basis_ref),
                (in_basis_hbm, in_basis_ref),
                (spectrum_hbm, spectrum_ref),
            )
        )
    ]
    for copy in loads:
        copy.start()

    barrier = pltpu.get_barrier_semaphore()

    def greet(step, carry):
        pl.semaphore_signal(
            barrier, inc=1, device_id=peer(lax.rem(me + step, n)), device_id_type=MESH
        )
        return carry

    lax.fori_loop(1, n, greet, 0)
    for step in range(1, groups):
        pl.semaphore_signal(barrier, inc=1, device_id=group_peer(step), device_id_type=MESH)

    mine = me // part_size
    place = lax.rem(me, part_size)

    def across(turn):
        return (1 - mine) * part_size + lax.rem(place + turn, part_size)

    def within(turn):
        return mine * part_size + lax.rem(place + part_size - turn, part_size)

    def source(turn):
        return (1 - mine) * part_size + lax.rem(place + part_size - turn, part_size)

    def near_source(turn):
        return mine * part_size + lax.rem(place + turn, part_size)

    def wanted(target, k):
        return jnp.maximum(slots_ref[target * slots + k], 0)

    loads[0].wait()
    loads[1].wait()
    load_train = [
        pltpu.make_async_copy(train_ref.at[k], train.at[k], train_sem.at[k]) for k in range(slots)
    ]
    for copy in load_train:
        copy.start()

    def fill(turn, carry):
        for k in range(slots):
            outgoing[turn, k] = query_ref[wanted(across(turn), k), pl.ds(group * share, share)]
        return carry

    lax.fori_loop(0, part_size, fill, 0)
    pl.semaphore_wait(barrier, n - 1 + groups - 1)

    def message(turn, k):
        return pltpu.make_async_remote_copy(
            src_ref=outgoing.at[turn, k],
            dst_ref=received.at[me, k, group],
            send_sem=send_sem.at[turn, k],
            recv_sem=recv_sem.at[turn, k],
            device_id=peer(across(turn)),
            device_id_type=MESH,
        )

    def near_message(turn, k):
        return pltpu.make_async_remote_copy(
            src_ref=direct.at[turn, k],
            dst_ref=received.at[me, k],
            send_sem=direct_send_sem.at[turn, k],
            recv_sem=direct_recv_sem.at[turn, k],
            device_id=peer(within(turn)),
            device_id_type=MESH,
        )

    def send(turn, carry):
        for k in range(slots):
            message(turn, k).start()
        return carry

    def send_near(turn, carry):
        for k in range(slots):
            for g in range(groups):
                direct[turn, k, g] = query_ref[wanted(within(turn), k), pl.ds(g * share, share)]
            near_message(turn, k).start()
            message(turn, k).start()
        return carry

    send(0, 0)
    lax.fori_loop(1, part_size, send_near, 0)
    for k in range(slots):
        for g in range(groups):
            received[me, k, g] = query_ref[wanted(me, k), pl.ds(g * share, share)]

    def arrival(turn, k):
        block = received.at[source(turn), k, group]
        return pltpu.make_async_remote_copy(
            src_ref=block,
            dst_ref=block,
            send_sem=send_sem.at[turn, k],
            recv_sem=recv_sem.at[turn, k],
            device_id=peer(source(turn)),
            device_id_type=MESH,
        )

    def near_arrival(turn, k):
        block = received.at[near_source(turn), k]
        return pltpu.make_async_remote_copy(
            src_ref=block,
            dst_ref=block,
            send_sem=direct_send_sem.at[turn, k],
            recv_sem=direct_recv_sem.at[turn, k],
            device_id=peer(near_source(turn)),
            device_id_type=MESH,
        )

    def hand_on(step, turn, k):
        block = received.at[source(turn), k, group]
        return pltpu.make_async_remote_copy(
            src_ref=block,
            dst_ref=block,
            send_sem=pass_sem.at[step, turn, k],
            recv_sem=passed_sem.at[step, turn, k],
            device_id=group_peer(step),
            device_id_type=MESH,
        )

    def handed(step, turn, k):
        giver = lax.rem(group + groups - step, groups)
        block = received.at[source(turn), k, giver]
        return pltpu.make_async_remote_copy(
            src_ref=block,
            dst_ref=block,
            send_sem=pass_sem.at[step, turn, k],
            recv_sem=passed_sem.at[step, turn, k],
            device_id=group_peer(step),
            device_id_type=MESH,
        )

    def turn_of(number):
        return number // slots, lax.rem(number, slots)

    def forward(number):
        turn, k = turn_of(number)
        arrival(turn, k).wait_recv()
        for step in range(1, groups):
            hand_on(step, turn, k).start()

    for copy in loads[2:]:
        copy.wait()

    for k in range(slots):
        u, v = out_basis_ref[k], in_basis_ref[k]
        for at, matrix in ((0, u.T), (1, u)):
            stacked = halves_below(matrix)
            left[k, at] = jnp.concatenate([stacked, stacked], axis=1)
        for at, matrix in ((0, v), (1, v.T)):
            beside = halves_beside(matrix)
            right[k, at] = jnp.concatenate([beside, beside], axis=0)
        module = slots_ref[me * slots + k]
        keep = jnp.where(module >= 0, ranks_ref[jnp.maximum(module, 0)], 0)
        spectrum = spectrum_ref[k]
        damping = 0.1 * jnp.mean(spectrum)
        kept = (lax.broadcasted_iota(jnp.int32, (dim, dim), 0) < keep) & (
            lax.broadcasted_iota(jnp.int32, (dim, dim), 1) < keep
        )
        weight = jnp.where(kept, 1.0 / (spectrum + damping), jnp.zeros_like(spectrum))
        weights[k] = jnp.concatenate([weight, weight], axis=1)

    def times_right(x, factor):
        product = jnp.dot(halves_beside(x), factor, preferred_element_type=F32)
        return product[:, :dim] + product[:, dim:]

    def times_left(factor, x):
        product = jnp.dot(factor, halves_below(x), preferred_element_type=F32)
        return product[:dim] + product[dim:]

    def side_by_side(x):
        return jnp.concatenate([x[:dim], x[dim:]], axis=1)

    def one_below_other(x):
        return jnp.concatenate([x[:, :dim], x[:, dim:]], axis=0)

    steps = examples // (2 * PAIRS)
    count = part_size * slots
    early = steps // 2 + (slots - 1) * steps

    for k in range(slots):
        load_train[k].wait()

        def rotate(step, carry, k=k):
            for pair in range(PAIRS):
                place = pl.ds((step * PAIRS + pair) * 2 * dim, 2 * dim)
                x = times_right(train[k, place], right[k, 0])
                x = times_left(left[k, 0], side_by_side(x)) * weights[k]
                x = times_right(one_below_other(x), right[k, 1])
                x = times_left(left[k, 1], side_by_side(x))
                train[k, place] = one_below_other(x)
            if k == 0:
                pl.when(lax.rem(step, 2) == 1)(lambda: forward(step // 2))
            else:
                forward(steps // 2 + (k - 1) * steps + step)
            return carry

        lax.fori_loop(0, steps, rotate, 0)

    total[...] = jnp.zeros_like(total)

    def score(origin, k):
        added = jnp.zeros_like(total)
        for row in range(0, rows, 2):
            asked, given = [], []
            for r in (row, row + 1):
                block = jnp.concatenate(
                    [received[origin, k, g, :, r, :] for g in range(groups)], axis=0
                )
                asked.append(halves_below(block))
                taken = train[k, pl.ds(origin * rows + r, examples, stride=dim), :]
                given.append(halves_below(taken))
            added += lax.dot_general(
                jnp.concatenate(asked, axis=1),
                jnp.concatenate(given, axis=1),
                (((1,), (1,)), ((), ())),
                preferred_element_type=F32,
            )
        total[...] += added

    def use(number):
        turn, k = turn_of(number)
        for step in range(1, groups):
            handed(step, turn, k).wait_recv()
        score(source(turn), k)

    for k in range(slots):
        score(me, k)

    late = count - early
    each = min(early // late, 3)
    near_count = (part_size - 1) * slots

    def use_near(number):
        turn, k = turn_of(number + slots)
        near_arrival(turn, k).wait_recv()
        score(near_source(turn), k)

    def late_forward(number, carry):
        forward(early + number)
        for at in range(each):
            use(each * number + at)
            if each == 3:
                use_near(each * number + at)
        return carry

    def near_only(number, carry):
        use_near(number)
        return carry

    def rest(number, carry):
        use(number)
        return carry

    lax.fori_loop(0, late, late_forward, 0)
    lax.fori_loop(late * each if each == 3 else 0, near_count, near_only, 0)
    lax.fori_loop(each * late, count, rest, 0)

    summed = total[...]
    summed = summed[:queries] + summed[queries:]
    summed = summed[:, :examples] + summed[:, examples:]
    half = queries // 2
    part[...] = jnp.concatenate([summed[:half], summed[half:]], axis=1)

    def partial(step):
        return pltpu.make_async_remote_copy(
            src_ref=part,
            dst_ref=parts.at[step],
            send_sem=sum_send_sem.at[step],
            recv_sem=sum_recv_sem.at[step],
            device_id=peer(lax.rem(me + step, n)),
            device_id_type=MESH,
        )

    def share_partial(step, carry):
        partial(step).start()
        return carry

    lax.fori_loop(1, n, share_partial, 0)
    parts[0] = part[...]

    def arrived(step, carry):
        partial(step).wait_recv()
        return carry

    lax.fori_loop(1, n, arrived, 0)

    def add(owner, running):
        return running + parts[lax.rem(me + n - owner, n)]

    final = lax.fori_loop(0, n, add, jnp.zeros_like(part))
    scores_ref[...] = jnp.concatenate([final[:, :examples], final[:, examples:]], axis=0)

    def drained(step, carry):
        partial(step).wait_send()
        return carry

    lax.fori_loop(1, n, drained, 0)

    def sent(turn, carry):
        for k in range(slots):
            message(turn, k).wait_send()
            for step in range(1, groups):
                hand_on(step, turn, k).wait_send()
        return carry

    def near_sent(turn, carry):
        for k in range(slots):
            near_message(turn, k).wait_send()
        return carry

    lax.fori_loop(0, part_size, sent, 0)
    lax.fori_loop(1, part_size, near_sent, 0)


def body(n, groups, query_grads, train_grads, out_basis, in_basis, corrections, ranks, slot_modules):
    modules, queries, rows, dim = query_grads.shape
    slots, examples = train_grads.shape[:2]
    share = queries // groups
    vmem = pl.BlockSpec(memory_space=pltpu.VMEM)
    hbm = pl.BlockSpec(memory_space=pltpu.HBM)
    return pl.pallas_call(
        functools.partial(kernel, n, groups),
        out_shape=jax.ShapeDtypeStruct((queries, examples), F32),
        in_specs=[hbm] * 7,
        out_specs=vmem,
        scratch_shapes=[
            pltpu.SMEM(slot_modules.shape, jnp.int32),
            pltpu.SMEM(ranks.shape, jnp.int32),
            pltpu.VMEM(query_grads.shape, F32),
            pltpu.VMEM(out_basis.shape, F32),
            pltpu.VMEM(in_basis.shape, F32),
            pltpu.VMEM(corrections.shape, F32),
            pltpu.VMEM((n // 2, slots, share, rows, dim), F32),
            pltpu.VMEM((n // 2, slots, groups, share, rows, dim), F32),
            pltpu.VMEM((n, slots, groups, share, rows, dim), F32),
            pltpu.VMEM((slots, examples * dim, dim), F32),
            pltpu.VMEM((slots, 2, 2 * dim, 2 * dim), BF16),
            pltpu.VMEM((slots, 2, 2 * dim, 2 * dim), BF16),
            pltpu.VMEM((slots, dim, 2 * dim), F32),
            pltpu.VMEM((2 * queries, 2 * examples), F32),
            pltpu.VMEM((queries // 2, 2 * examples), F32),
            pltpu.VMEM((n, queries // 2, 2 * examples), F32),
            pltpu.SemaphoreType.DMA((6,)),
            pltpu.SemaphoreType.DMA((slots,)),
            pltpu.SemaphoreType.DMA((n // 2, slots)),
            pltpu.SemaphoreType.DMA((n // 2, slots)),
            pltpu.SemaphoreType.DMA((n // 2, slots)),
            pltpu.SemaphoreType.DMA((n // 2, slots)),
            pltpu.SemaphoreType.DMA((groups, n // 2, slots)),
            pltpu.SemaphoreType.DMA((groups, n // 2, slots)),
            pltpu.SemaphoreType.DMA((n,)),
            pltpu.SemaphoreType.DMA((n,)),
        ],
        compiler_params=pltpu.CompilerParams(
            collective_id=0, has_side_effects=True, vmem_limit_bytes=64 * 1024 * 1024
        ),
    )(
        slot_modules, ranks, query_grads, train_grads.reshape(slots, examples * dim, dim),
        out_basis, in_basis, corrections,
    )


def solution(mesh):
    return jax.shard_map(
        functools.partial(body, mesh.shape["module"], mesh.shape["group"]),
        mesh=mesh,
        in_specs=(
            P(None, None, "module", None),
            P("module", "group", None, None),
            P("module", None, None),
            P("module", None, None),
            P("module", None, None),
            P(),
            P(),
        ),
        out_specs=P(None, "group"),
        check_vma=False,
    )
```
